32 devices in a mesh: lon: 16 (over z, x, core), lat: 2 (over y).
Axes of the slice: x: 2, y: 2, z: 4, core: 2. Of those that a mesh axis runs over, the one named last changes fastest.
Arguments:
- field: bfloat16 [8, 512, 256], P('lat', 'lon'), may hold values from -6 to 6
- cotangent: bfloat16 [8, 512, 256], P('lat', 'lon'), may hold values from -6 to 6
- mix_weight: bfloat16 [256, 256], replicated, may hold values from -0.375 to 0.375
- first_weight: float32 [3, 256], replicated, may hold values from -0.34 to 0.34
- first_bias: float32 [256], replicated, may hold values from -0.5 to 0.5
- hidden_weight: bfloat16 [256, 256], replicated, may hold values from -0.375 to 0.375
- hidden_bias: float32 [256], replicated, may hold values from -1 to 1
- output_weight: bfloat16 [256, 256], replicated, may hold values from -0.375 to 0.375
- output_bias: float32 [256], replicated, may hold values from -0.5 to 0.5
- lon_half: int32 [8], replicated, may hold values from 3 to 32, as said below
- lat_half: int32 [8], replicated, may hold values from 1 to 4, as said below
Outputs:
- grad_field: bfloat16 [8, 512, 256], P('lat', 'lon')
- grad_mix: float32 [256, 256], replicated
- grad_first_weight: float32 [3, 256], replicated
- grad_first_bias: float32 [256], replicated
- grad_hidden_weight: float32 [256, 256], replicated
- grad_hidden_bias: float32 [256], replicated
- grad_output_weight: float32 [256, 256], replicated
- grad_output_bias: float32 [256], replicated
The draws below stay inside these ranges and needn't reach their ends.
Inputs may be any that keep to these rules, and one draw needn't show every extreme that they name: lon_half[i] is row i's half-width in longitude: 32 in the first and last rows. lat_half[i] is row i's half-width in latitude: 4 in the first and last rows.
All inputs are finite; a program needn't handle non-finite values.
Results may differ from the reference program's by a relative error of at most 0.0064.
Values may be sent and summed in bfloat16 or wider, within the bound.
A program may use at most 128 MiB of HBM per device.

```python
import math
import jax
import jax.numpy as jnp
from jax import lax

C = 256
HID = 256
HLON = 32
HLAT = 4
NLAT = 8
NLON = 512


def edge_distance():
    row_index = jnp.arange(NLAT)
    return jnp.minimum(row_index, NLAT - 1 - row_index)


def draw_lon_half(key, part):
    distance = edge_distance()
    widths = 3 * NLAT // (2 * distance + 1)
    jitter = jax.random.randint(jax.random.fold_in(key, 11), (NLAT,), 0, 5)
    widths = jnp.clip(widths + jitter, 3, HLON)
    return jnp.where(distance == 0, HLON, widths).astype(jnp.int32)


def draw_lat_half(key, part):
    distance = edge_distance()
    widths = jax.random.randint(jax.random.fold_in(key, 23), (NLAT,), 1, HLAT + 1)
    return jnp.where(distance == 0, HLAT, widths).astype(jnp.int32)


def block_scale(stream_key, dims, split, smallest, largest):
    def one(position, parts):
        heights = jax.random.uniform(jax.random.fold_in(jax.random.fold_in(stream_key, 6), position), (parts,), jnp.float32, smallest / len(split), largest / len(split))
        return jnp.repeat(jnp.exp(heights), dims[position] // parts).reshape((-1,) + (1,) * (len(dims) - position - 1))

    factor_of = one(*split[0])
    for cut in split[1:]:
        factor_of = factor_of * one(*cut)
    return factor_of


def gaussian(stream_key, dims, scale, limit, cuts=(), dtype=jnp.bfloat16):
    values = scale * jax.random.normal(stream_key, dims, jnp.float32)
    if cuts:
        values = values * block_scale(stream_key, dims, cuts, -0.22, 0.18)
    return jnp.clip(values, -limit, limit).astype(dtype)


def setup_inputs(seed: int = 0) -> dict:
    key_of = jax.random.split(jax.random.key(seed), 12)
    field = gaussian(key_of[0], (NLAT, NLON, C), 1.0, 6.0, ((0, 2), (1, 16)))
    cotangent = gaussian(key_of[1], (NLAT, NLON, C), 1.0, 6.0, ((0, 2), (1, 16)))
    mix_weight = gaussian(key_of[2], (C, C), C ** -0.5, 0.375)
    first_weight = jnp.clip(jax.random.uniform(key_of[3], (3, HID), jnp.float32, -0.34, 0.34), -0.34, 0.34)
    first_bias = jnp.clip(jax.random.uniform(key_of[4], (HID,), jnp.float32, -0.5, 0.5), -0.5, 0.5)
    hidden_weight = gaussian(key_of[5], (HID, HID), HID ** -0.5, 0.375)
    hidden_bias = jnp.clip(jax.random.uniform(key_of[6], (HID,), jnp.float32, -1.0, 1.0), -1.0, 1.0)
    output_weight = gaussian(key_of[7], (HID, C), HID ** -0.5, 0.375)
    output_bias = jnp.clip(jax.random.uniform(key_of[8], (C,), jnp.float32, -0.5, 0.5), -0.5, 0.5)
    lon_half = draw_lon_half(jax.random.fold_in(key_of[11], 71), 0)
    lat_half = draw_lat_half(jax.random.fold_in(key_of[11], 71), 0)
    return dict(field=field, cotangent=cotangent, mix_weight=mix_weight, first_weight=first_weight, first_bias=first_bias, hidden_weight=hidden_weight, hidden_bias=hidden_bias, output_weight=output_weight, output_bias=output_bias, lon_half=lon_half, lat_half=lat_half)


first_omega = 30.0

def tap_setup(lon_half, lat_half):
    taps_lon = 2 * HLON + 1
    taps_lat = 2 * HLAT + 1
    row_index = jnp.arange(NLAT).astype(jnp.float32)
    shift_lon = jnp.arange(taps_lon) - HLON
    shift_lat = jnp.arange(taps_lat) - HLAT
    half_lon = lon_half[:, None, None]
    half_lat = lat_half[:, None, None]
    shape = (NLAT, taps_lon, taps_lat)
    lon_coord = jnp.broadcast_to(shift_lon[None, :, None].astype(jnp.float32) / half_lon.astype(jnp.float32), shape)
    lat_coord = jnp.broadcast_to(shift_lat[None, None, :].astype(jnp.float32) / half_lat.astype(jnp.float32), shape)
    lat_sine = jnp.broadcast_to(jnp.sin(jnp.pi * ((row_index + 0.5) / NLAT - 0.5))[:, None, None], shape)
    inside = (jnp.abs(shift_lon)[None, :, None] <= half_lon) & (jnp.abs(shift_lat)[None, None, :] <= half_lat)
    row_norm = lax.rsqrt(((2 * lon_half + 1) * (2 * lat_half + 1)).astype(jnp.float32))
    tap_scale = jnp.where(inside, jnp.broadcast_to(row_norm[:, None, None], shape), jnp.zeros(shape, jnp.float32))
    return (lon_coord, lat_coord, lat_sine, tap_scale)

def reference(field, cotangent, mix_weight, first_weight, first_bias, hidden_weight, hidden_bias, output_weight, output_bias, lon_half, lat_half):
    highest = lax.Precision.HIGHEST
    taps_lon = 2 * HLON + 1
    taps_lat = 2 * HLAT + 1
    lon_coord, lat_coord, lat_sine, tap_scale = tap_setup(lon_half, lat_half)
    pre_first = lon_coord[..., None] * first_weight[0] + lat_coord[..., None] * first_weight[1] + lat_sine[..., None] * first_weight[2] + first_bias
    pre_first = pre_first.reshape(-1, HID)
    hidden_first = jnp.sin(first_omega * pre_first).astype(jnp.bfloat16)
    pre_hidden = jnp.dot(hidden_first, hidden_weight, preferred_element_type=jnp.float32) + hidden_bias
    hidden_second = jnp.sin(pre_hidden).astype(jnp.bfloat16)
    raw_kernel = jnp.dot(hidden_second, output_weight, preferred_element_type=jnp.float32) + output_bias
    kernel = (raw_kernel.reshape(NLAT, taps_lon, taps_lat, C) * tap_scale[..., None]).astype(jnp.bfloat16)
    flat_cot = cotangent.reshape(-1, C)
    mixed_cot = lax.dot_general(flat_cot, mix_weight, (((1,), (1,)), ((), ())), preferred_element_type=jnp.float32).astype(jnp.bfloat16).reshape(NLAT, NLON, C)
    row_pad = ((HLAT, HLAT), (0, 0), (0, 0))
    field_rows = jnp.pad(field, row_pad)
    cot_rows = jnp.pad(mixed_cot, row_pad)
    kernel_rows = jnp.pad(kernel, ((HLAT, HLAT), (0, 0), (0, 0), (0, 0)))
    cot_float = mixed_cot.astype(jnp.float32)

    def one_tap(carry, column):
        conv_total, back_total = carry
        offset = column - HLON
        field_moved = jnp.roll(field_rows, -offset, axis=1)
        cot_moved = jnp.roll(cot_rows, offset, axis=1)
        kernel_col = lax.dynamic_index_in_dim(kernel, column, 1, keepdims=False)
        kernel_ext = lax.dynamic_index_in_dim(kernel_rows, column, 1, keepdims=False)
        pieces = []
        for a in range(taps_lat):
            source = field_moved[a:a + NLAT].astype(jnp.float32)
            conv_total = conv_total + source * kernel_col[:, a][:, None, :].astype(jnp.float32)
            pieces.append(lax.optimization_barrier(jnp.sum(source * cot_float, axis=1)))
            row_from = 2 * HLAT - a
            back_total = back_total + cot_moved[row_from:row_from + NLAT].astype(jnp.float32) * kernel_ext[row_from:row_from + NLAT, a][:, None, :].astype(jnp.float32)
        return ((conv_total, back_total), jnp.stack(pieces, axis=1))
    zeros = jnp.zeros((NLAT, NLON, C), jnp.float32)
    (conv_total, back_total), tap_grads = lax.scan(one_tap, (zeros, zeros), jnp.arange(taps_lon))
    grad_kernel = jnp.transpose(tap_grads, (1, 0, 2, 3))
    conv_out = conv_total.astype(jnp.bfloat16)
    grad_field = back_total.astype(jnp.bfloat16)
    inverse = 1.0 / math.sqrt(NLAT * NLON)
    grad_mix = lax.dot_general(conv_out.reshape(-1, C), flat_cot, (((0,), (0,)), ((), ())), preferred_element_type=jnp.float32) * inverse
    grad_raw = (grad_kernel * tap_scale[..., None]).reshape(-1, C)
    grad_output_weight = jnp.dot(hidden_second.astype(jnp.float32).T, grad_raw, precision=highest) * inverse
    grad_output_bias = lax.optimization_barrier(jnp.sum(grad_raw, axis=0)) * inverse
    grad_pre_hidden = jnp.dot(grad_raw, output_weight.astype(jnp.float32).T, precision=highest) * jnp.cos(pre_hidden)
    grad_hidden_weight = jnp.dot(hidden_first.astype(jnp.float32).T, grad_pre_hidden, precision=highest) * inverse
    grad_hidden_bias = lax.optimization_barrier(jnp.sum(grad_pre_hidden, axis=0)) * inverse
    grad_pre_first = first_omega * jnp.dot(grad_pre_hidden, hidden_weight.astype(jnp.float32).T, precision=highest) * jnp.cos(first_omega * pre_first)
    features = jnp.stack((lon_coord.reshape(-1), lat_coord.reshape(-1), lat_sine.reshape(-1)), axis=0)
    grad_first_weight = jnp.dot(features, grad_pre_first, precision=highest) * inverse
    grad_first_bias = lax.optimization_barrier(jnp.sum(grad_pre_first, axis=0)) * inverse
    return (grad_field, grad_mix, grad_first_weight, grad_first_bias, grad_hidden_weight, grad_hidden_bias, grad_output_weight, grad_output_bias)
```

```python
import math

import jax
import jax.numpy as jnp
import numpy as np
from jax import lax
from jax.experimental import pallas as pl
from jax.experimental.pallas import tpu as pltpu
from jax.sharding import PartitionSpec as P

HLON = 32
HLAT = 4
TAPS_LAT = 2 * HLAT + 1
GROUP = 8
CENTRE = HLON + 4
TAPS_LON = 2 * CENTRE
LANES = 128
SUBLANES = 8

first_omega = 30.0

_nodes = (1.0 - np.cos(np.pi * (np.arange(400) + 0.5) / 400)) / 8.0
COS_COEFFS = [
    float(c) for c in np.polynomial.polynomial.polyfit(_nodes, np.cos(2 * np.pi * np.sqrt(_nodes)), 6)
]


def cos_turns(turns):
    rest = turns - jnp.round(turns)
    square = rest * rest
    total = jnp.full_like(square, COS_COEFFS[-1])
    for coeff in COS_COEFFS[-2::-1]:
        total = total * square + coeff
    return total


def halo(block, lat_count, lon_count):
    def shifted(up, right):
        pairs = []
        for lat in range(lat_count):
            for lon in range(lon_count):
                to_lat = lat + up
                if 0 <= to_lat < lat_count:
                    to_lon = (lon + right) % lon_count
                    pairs.append((lon * lat_count + lat, to_lon * lat_count + to_lat))
        return lax.ppermute(block, ("lon", "lat"), pairs)

    rows = []
    for up in (1, 0, -1):
        parts = [block if (up, right) == (0, 0) else shifted(up, right) for right in (1, 0, -1)]
        rows.append(jnp.concatenate(parts, axis=1))
    return jnp.concatenate(rows, axis=0)


def fill_windows(source_ref, windows, step):
    def one_row(row, _):
        for h in range(source_ref.shape[1]):
            for p in range(windows.shape[2]):
                windows[row, h, p] = source_ref[row, h, pl.ds(p, SUBLANES, stride=step), :]
        return 0

    lax.fori_loop(0, source_ref.shape[0], one_row, 0)


def forward_kernel(low_ref, high_ref, field_ref, cot_ref, kern_ref, conv_ref, grad_ref, windows):
    rows, halves, cols, _ = cot_ref.shape
    step = cols // SUBLANES
    fill_windows(field_ref, windows, step)
    slots = [(h, l) for h in range(halves) for l in range(step)]

    def one_row(row, _):
        cot = [cot_ref[row, h, pl.ds(l, SUBLANES, stride=step), :] for h, l in slots]

        def one_lat(a, acc):
            pair = row * TAPS_LAT + a

            def one_group(group, acc):
                acc = list(acc)
                first = pl.multiple_of(group * GROUP, GROUP)
                for h in range(halves):
                    lanes = pl.ds(h * LANES, LANES)
                    view = [windows[row + a, h, first + q] for q in range(GROUP + step - 1)]
                    taps = kern_ref[pair, pl.ds(first, GROUP), lanes]
                    sums = []
                    for t in range(GROUP):
                        kern = jnp.broadcast_to(taps[t : t + 1], (SUBLANES, LANES))
                        part = None
                        for l in range(step):
                            slot = h * step + l
                            acc[slot] = acc[slot] + view[t + l] * kern
                            term = view[t + l] * cot[slot]
                            part = term if part is None else part + term
                        sums.append(jnp.sum(part, axis=0, keepdims=True))
                    grad_ref[pair, pl.ds(first, GROUP), lanes] = jnp.concatenate(sums, axis=0)
                return tuple(acc)

            return lax.fori_loop(low_ref[pair], high_ref[pair], one_group, acc)

        zero = jnp.zeros((SUBLANES, LANES), jnp.float32)
        acc = lax.fori_loop(0, TAPS_LAT, one_lat, (zero,) * len(slots))
        for (h, l), value in zip(slots, acc):
            conv_ref[row, h, pl.ds(l, SUBLANES, stride=step), :] = value
        return 0

    lax.fori_loop(0, rows, one_row, 0)


def backward_kernel(low_ref, high_ref, pair_ref, cot_ref, kern_ref, out_ref, windows):
    rows, halves, cols, _ = out_ref.shape
    step = cols // SUBLANES
    fill_windows(cot_ref, windows, step)
    slots = [(h, l) for h in range(halves) for l in range(step)]

    def one_row(row, _):
        def one_lat(a, acc):
            entry = row * TAPS_LAT + a
            pair = pair_ref[entry]
            source = row + 2 * HLAT - a

            def one_group(group, acc):
                acc = list(acc)
                first = pl.multiple_of(group * GROUP, GROUP)
                base = TAPS_LON - first - (GROUP - 1)
                for h in range(halves):
                    lanes = pl.ds(h * LANES, LANES)
                    view = [windows[source, h, base + q] for q in range(GROUP + step - 1)]
                    taps = kern_ref[pair, pl.ds(first, GROUP), lanes]
                    for t in range(GROUP):
                        kern = jnp.broadcast_to(taps[t : t + 1], (SUBLANES, LANES))
                        for l in range(step):
                            slot = h * step + l
                            acc[slot] = acc[slot] + view[GROUP - 1 - t + l] * kern
                return tuple(acc)

            return lax.fori_loop(low_ref[entry], high_ref[entry], one_group, acc)

        zero = jnp.zeros((SUBLANES, LANES), jnp.float32)
        acc = lax.fori_loop(0, TAPS_LAT, one_lat, (zero,) * len(slots))
        for (h, l), value in zip(slots, acc):
            out_ref[row, h, pl.ds(l, SUBLANES, stride=step), :] = value
        return 0

    lax.fori_loop(0, rows, one_row, 0)


def split_lanes(block):
    rows, cols, channels = block.shape
    return block.reshape(rows, cols, channels // LANES, LANES).transpose(0, 2, 1, 3)


def join_lanes(block):
    rows, halves, cols, _ = block.shape
    return block.transpose(0, 2, 1, 3).reshape(rows, cols, halves * LANES)


def tap_pairs(lat_rows):
    pairs = [(HLAT + i, a) for i in range(lat_rows) for a in range(TAPS_LAT)]
    place = {pair: k for k, pair in enumerate(pairs)}
    table = []
    for row in range(lat_rows):
        for a in range(TAPS_LAT):
            pair = (row + 2 * HLAT - a, a)
            if pair not in place:
                place[pair] = len(pairs)
                pairs.append(pair)
            table.append(place[pair])
    return np.array(pairs, np.int32), np.array(table, np.int32)


def shards(
    field,
    cotangent,
    mix_weight,
    first_weight,
    first_bias,
    hidden_weight,
    hidden_bias,
    output_weight,
    output_bias,
    lon_half,
    lat_half,
):
    lat_rows, lon_cols, channels = field.shape
    lat_count = lax.axis_size("lat")
    lon_count = lax.axis_size("lon")
    grid_rows = lat_rows * lat_count
    grid_cols = lon_cols * lon_count
    halves = channels // LANES
    row_start = lax.axis_index("lat") * lat_rows
    flat_cot = cotangent.reshape(-1, channels)
    mixed_cot = lax.dot_general(
        flat_cot, mix_weight, (((1,), (1,)), ((), ())), preferred_element_type=jnp.float32
    ).astype(jnp.bfloat16)
    mixed_cot = mixed_cot.reshape(lat_rows, lon_cols, channels)
    field_ext = halo(field, lat_count, lon_count)
    cot_ext = halo(mixed_cot, lat_count, lon_count)

    def padded(block):
        row_skip = lat_rows - HLAT
        col_skip = lon_cols - HLON
        block = block[row_skip : row_skip + lat_rows + 2 * HLAT]
        block = block[:, col_skip : col_skip + lon_cols + 2 * HLON].astype(jnp.float32)
        extra = CENTRE - HLON
        return split_lanes(jnp.pad(block, ((0, 0), (extra, extra), (0, 0))))

    field_pad = padded(field_ext)
    cot_pad = padded(cot_ext)

    pairs, table = tap_pairs(lat_rows)
    own = lat_rows * TAPS_LAT
    pair_row = row_start - HLAT + pairs[:, 0]
    in_grid = (pair_row >= 0) & (pair_row < grid_rows)
    safe_row = jnp.clip(pair_row, 0, grid_rows - 1)
    half_lon = lon_half[safe_row]
    half_lat = lat_half[safe_row]
    shift_lat = jnp.asarray(pairs[:, 1] - HLAT)
    used = in_grid & (jnp.abs(shift_lat) <= half_lat)
    low = (CENTRE - half_lon) // GROUP
    high = jnp.where(used, (CENTRE + half_lon) // GROUP + 1, low)
    target = pair_row + shift_lat
    forward_high = jnp.where((target >= 0) & (target < grid_rows), high, low)[:own]
    forward_low = low[:own]
    back_low = low[table]
    back_high = high[table]

    shift_lon = jnp.arange(TAPS_LON) - CENTRE
    lon_coord = shift_lon[None, :].astype(jnp.float32) / half_lon[:, None].astype(jnp.float32)
    lat_coord = shift_lat.astype(jnp.float32) / half_lat.astype(jnp.float32)
    lat_sine = jnp.sin(jnp.pi * ((safe_row.astype(jnp.float32) + 0.5) / grid_rows - 0.5))
    inside = (jnp.abs(shift_lon)[None, :] <= half_lon[:, None]) & used[:, None]
    row_norm = lax.rsqrt(((2 * half_lon + 1) * (2 * half_lat + 1)).astype(jnp.float32))
    tap_scale = jnp.where(inside, row_norm[:, None], 0.0)
    per_pair = (
        lat_coord[:, None] * first_weight[1] + lat_sine[:, None] * first_weight[2] + first_bias
    )
    scale_first = first_omega / (2 * math.pi)
    turns_first = (
        lon_coord[:, :, None] * (first_weight[0] * scale_first)
        + (per_pair * scale_first)[:, None, :]
    ).reshape(-1, first_weight.shape[1])
    hidden_first = cos_turns(turns_first - 0.25).astype(jnp.bfloat16)
    turns_hidden = (
        jnp.dot(hidden_first, hidden_weight, preferred_element_type=jnp.float32) + hidden_bias
    ) * (1.0 / (2 * math.pi))
    hidden_second = cos_turns(turns_hidden - 0.25).astype(jnp.bfloat16)
    raw_kernel = (
        jnp.dot(hidden_second, output_weight, preferred_element_type=jnp.float32) + output_bias
    )
    kernel = raw_kernel.reshape(pairs.shape[0], TAPS_LON, channels) * tap_scale[:, :, None]
    kernel = kernel.astype(jnp.bfloat16).astype(jnp.float32)

    smem = pl.BlockSpec(memory_space=pltpu.SMEM)
    vmem = pl.BlockSpec(memory_space=pltpu.VMEM)
    window_rows = lat_rows + 2 * HLAT
    windows = pltpu.VMEM(
        (window_rows, halves, TAPS_LON + lon_cols // SUBLANES, SUBLANES, LANES), jnp.float32
    )
    params = pltpu.CompilerParams(vmem_limit_bytes=48 * 1024 * 1024)
    rows_shape = jax.ShapeDtypeStruct((lat_rows, halves, lon_cols, LANES), jnp.float32)
    conv, grad_kernel = pl.pallas_call(
        forward_kernel,
        out_shape=(rows_shape, jax.ShapeDtypeStruct((own, TAPS_LON, channels), jnp.float32)),
        in_specs=[smem, smem, vmem, vmem, vmem],
        out_specs=(vmem, vmem),
        scratch_shapes=[windows],
        compiler_params=params,
        name="conv_and_kernel_grad",
    )(
        forward_low,
        forward_high,
        field_pad,
        split_lanes(mixed_cot.astype(jnp.float32)),
        kernel[:own],
    )
    back = pl.pallas_call(
        backward_kernel,
        out_shape=rows_shape,
        in_specs=[smem, smem, smem, vmem, vmem],
        out_specs=vmem,
        scratch_shapes=[windows],
        compiler_params=params,
        name="field_grad",
    )(back_low, back_high, jnp.asarray(table), cot_pad, kernel)
    grad_field = join_lanes(back.astype(jnp.bfloat16))

    conv_out = join_lanes(conv.astype(jnp.bfloat16))
    grad_mix = lax.dot_general(
        conv_out.reshape(-1, channels),
        flat_cot,
        (((0,), (0,)), ((), ())),
        preferred_element_type=jnp.float32,
    )

    count = own * TAPS_LON
    reached = (jnp.arange(TAPS_LON)[None, :] >= forward_low[:, None] * GROUP) & (
        jnp.arange(TAPS_LON)[None, :] < forward_high[:, None] * GROUP
    )
    grad_raw = jnp.where(
        (inside[:own] & reached)[:, :, None], grad_kernel * tap_scale[:own, :, None], 0.0
    ).reshape(count, channels)
    raw_half = grad_raw.astype(jnp.bfloat16)

    def over_taps(left, right):
        return lax.dot_general(
            left, right, (((0,), (0,)), ((), ())), preferred_element_type=jnp.float32
        )

    def back_through(grad, weight):
        return lax.dot_general(
            grad, weight, (((1,), (1,)), ((), ())), preferred_element_type=jnp.float32
        )

    grad_output_weight = over_taps(hidden_second[:count], raw_half)
    grad_output_bias = jnp.sum(grad_raw, axis=0)
    grad_pre_hidden = back_through(raw_half, output_weight) * cos_turns(turns_hidden[:count])
    hidden_half = grad_pre_hidden.astype(jnp.bfloat16)
    grad_hidden_weight = over_taps(hidden_first[:count], hidden_half)
    grad_hidden_bias = jnp.sum(grad_pre_hidden, axis=0)
    grad_pre_first = (
        first_omega * back_through(hidden_half, hidden_weight) * cos_turns(turns_first[:count])
    )
    ones = jnp.ones((own, TAPS_LON), jnp.float32)
    features = jnp.stack(
        (lon_coord[:own], lat_coord[:own, None] * ones, lat_sine[:own, None] * ones, ones), axis=0
    ).reshape(4, count)
    grad_first = jnp.dot(features, grad_pre_first, precision=lax.Precision.HIGHEST)

    inverse = 1.0 / math.sqrt(grid_rows * grid_cols)
    packed = jnp.concatenate(
        (
            grad_mix,
            grad_hidden_weight,
            grad_output_weight,
            grad_first,
            grad_hidden_bias[None],
            grad_output_bias[None],
            jnp.zeros((2, channels), jnp.float32),
        ),
        axis=0,
    )
    summed = lax.psum(packed * inverse, ("lon", "lat"))
    c = channels
    return (
        grad_field,
        summed[:c],
        summed[3 * c : 3 * c + 3],
        summed[3 * c + 3],
        summed[c : 2 * c],
        summed[3 * c + 4],
        summed[2 * c : 3 * c],
        summed[3 * c + 5],
    )


def solution(mesh):
    in_specs = (
        P("lat", "lon", None),
        P("lat", "lon", None),
        P(),
        P(),
        P(),
        P(),
        P(),
        P(),
        P(),
        P(),
        P(),
    )
    out_specs = (P("lat", "lon", None), P(), P(), P(), P(), P(), P(), P())
    return jax.shard_map(shards, mesh=mesh, in_specs=in_specs, out_specs=out_specs, check_vma=False)
```
